32 devices in a mesh: ctx: 8 (over z, x), head: 4 (over y, core).
Axes of the slice: x: 2, y: 2, z: 4, core: 2. Of those that a mesh axis runs over, the one named last changes fastest.
Arguments:
- queries: bfloat16 [2048, 4096], P(('ctx', 'head')), may hold values from -200 to 200
- keys: bfloat16 [2048, 512], P(('ctx', 'head')), may hold values from -6 to 6
- values: bfloat16 [2048, 512], P(('ctx', 'head')), may hold values from -6 to 6
Outputs:
- attended: bfloat16 [2048, 4096], P(('ctx', 'head'))
The draws below stay inside these ranges and needn't reach their ends.
All inputs are finite; a program needn't handle non-finite values.
Results may differ from the reference program's by a relative error of at most 0.0065.
Values may be sent and summed in bfloat16 or wider, within the bound.
No kernel may reach another device: no remote copies, remote signals or barrier semaphores. Data moves between devices by JAX's collectives and lax.ppermute only.
A program may use at most 64 MiB of HBM per device.

```python
import math
import jax
import jax.numpy as jnp
from jax import lax

QH = 32
KVH = 4
HD = 128
TOKENS = 2048


def base_keys(key):
    return jnp.clip(jax.random.normal(key, (TOKENS, KVH, HD), jnp.float32), -6.0, 6.0)


def draw_keys(key, part):
    shared = base_keys(key)
    return shared.reshape(TOKENS, KVH * HD).astype(jnp.bfloat16)


def draw_queries(key, part):
    key = jax.random.fold_in(key, 7)
    own = jnp.clip(jax.random.normal(key, (TOKENS, QH, HD), jnp.float32), -6.0, 6.0)
    return own.reshape(TOKENS, QH * HD).astype(jnp.bfloat16)


def block_scale(rng, shape, pieces, least, top_value):
    gain = 1.0
    for axis_at, shards_of in pieces:
        steps = jax.random.uniform(jax.random.fold_in(jax.random.fold_in(rng, 6), axis_at), (shards_of,), jnp.float32, least / len(pieces), top_value / len(pieces))
        gain = gain * jnp.repeat(jnp.exp(steps), shape[axis_at] // shards_of).reshape((-1,) + (1,) * (len(shape) - 1 - axis_at))
    return gain


def normal_values(stream_key, extent, width, limit, cuts=(), held_as=jnp.bfloat16):
    values = width * jax.random.normal(stream_key, extent, jnp.float32)
    if cuts:
        values = values * block_scale(stream_key, extent, cuts, -0.22, 0.18)
    return jnp.clip(values, -limit, limit).astype(held_as)


def setup_inputs(seed: int = 0) -> dict:
    seeds = jax.random.split(jax.random.key(seed), 4)
    queries = draw_queries(jax.random.fold_in(seeds[3], 71), 0)
    keys = draw_keys(jax.random.fold_in(seeds[3], 71), 0)
    values = normal_values(seeds[2], (TOKENS, KVH * HD), 1.0, 6.0, ((0, 32),))
    return {"queries": queries, "keys": keys, "values": values}


def reference(queries, keys, values):
    group = QH // KVH
    scale = 1.0 / math.sqrt(HD)
    query_all = queries.reshape(TOKENS, KVH, group, HD).transpose(1, 0, 2, 3)
    key_all = keys.reshape(TOKENS, KVH, HD).transpose(1, 0, 2)
    value_all = values.reshape(TOKENS, KVH, HD).transpose(1, 0, 2)
    block = math.gcd(TOKENS, 1024)
    count = TOKENS // block
    key_pos = jnp.arange(TOKENS, dtype=jnp.int32)

    def per_head(inputs):
        query_head, key_head, value_head = inputs
        key_float = key_head.astype(jnp.float32)
        value_float = value_head.astype(jnp.float32)

        def per_block(index):
            first = (index * block).astype(jnp.int32)
            query_rows = lax.dynamic_slice_in_dim(query_head, first, block, 0).astype(jnp.float32)
            scores = jnp.einsum('tgd,kd->gtk', query_rows, key_float) * scale
            query_pos = first + jnp.arange(block, dtype=jnp.int32)
            allowed = query_pos[:, None] >= key_pos[None, :]
            scores = jnp.where(allowed, scores, -1e+30)
            peak = lax.optimization_barrier(jnp.max(scores, axis=-1, keepdims=True))
            weights = jnp.exp(scores - peak)
            totals = lax.optimization_barrier(jnp.sum(weights, axis=-1))
            rounded = lax.optimization_barrier(weights.astype(jnp.bfloat16)).astype(jnp.float32)
            summed = jnp.einsum('gtk,kd->tgd', rounded, value_float)
            return (summed / totals.T[:, :, None]).astype(jnp.bfloat16)
        return lax.map(per_block, jnp.arange(count, dtype=jnp.int32))
    outputs = lax.map(per_head, (query_all, key_all, value_all))
    return outputs.transpose(1, 2, 0, 3, 4).reshape(TOKENS, QH * HD)
```

```python
import functools
import math

import jax
import jax.numpy as jnp
from jax import lax
from jax.experimental import pallas as pl
from jax.experimental.pallas import tpu as pltpu
from jax.sharding import PartitionSpec as P

QH = 32
KVH = 4
HD = 128
GROUP = QH // KVH
AXES = ("ctx", "head")
PLANE = 8
FAR = -1e30
FAR_PLACE = 2**30
FACTOR = math.log2(math.e) / math.sqrt(HD)
VMEM = pl.BlockSpec(memory_space=pltpu.VMEM)
FREE = pl.CostEstimate(flops=0, bytes_accessed=0, transcendentals=0)


def pack_kernel(keys_ref, values_ref, out_ref, sems):
    width = keys_ref.shape[1]
    copies = [
        pltpu.make_async_copy(keys_ref, out_ref.at[:, :width], sems.at[0]),
        pltpu.make_async_copy(values_ref, out_ref.at[:, width:], sems.at[1]),
    ]
    for copy in copies:
        copy.start()
    for copy in copies:
        copy.wait()


def pack(keys, values):
    rows, width = keys.shape
    return pl.pallas_call(
        pack_kernel,
        out_shape=jax.ShapeDtypeStruct((rows, 2 * width), keys.dtype),
        in_specs=[pl.BlockSpec(memory_space=pltpu.HBM)] * 2,
        out_specs=VMEM,
        scratch_shapes=[pltpu.SemaphoreType.DMA((2,))],
        compiler_params=pltpu.CompilerParams(vmem_limit_bytes=2 * 2**20),
        name="pack",
    )(keys, values)


def join_kernel(a_ref, b_ref, *refs):
    rows, out_ref = a_ref.shape[0], refs[-1]
    out_ref[:rows] = a_ref[...]
    out_ref[rows:] = b_ref[...]


def join(a, b, after=()):
    return pl.pallas_call(
        join_kernel,
        out_shape=jax.ShapeDtypeStruct((2 * a.shape[0], a.shape[1]), a.dtype),
        in_specs=[VMEM] * 2 + [pl.BlockSpec(memory_space=pl.ANY)] * len(after),
        out_specs=VMEM,
        compiler_params=pltpu.CompilerParams(vmem_limit_bytes=2 * 2**20),
        cost_estimate=FREE,
        name="join",
    )(a, b, *after)


def hold_kernel(block_ref, *refs):
    refs[-1][...] = block_ref[...]


def hold(block, after=()):
    return pl.pallas_call(
        hold_kernel,
        out_shape=jax.ShapeDtypeStruct(block.shape, block.dtype),
        in_specs=[VMEM] + [pl.BlockSpec(memory_space=pl.ANY)] * len(after),
        out_specs=VMEM,
        compiler_params=pltpu.CompilerParams(vmem_limit_bytes=2 * 2**20),
        cost_estimate=FREE,
        name="hold",
    )(block, *after)


def columns(blocks, at):
    return jnp.concatenate([b[:, at : at + HD] for b in blocks], axis=0)


def lane_groups(scores):
    return [scores[:, at : at + HD] for at in range(0, scores.shape[1], HD)]


def fold_head(h, q_ref, blocks, allowed, state):
    queries = jnp.concatenate(
        [q_ref[:, (h * GROUP + g) * HD : (h * GROUP + g + 1) * HD] for g in range(GROUP)], axis=0
    )
    keys = columns(blocks, h * HD)
    values = columns(blocks, (KVH + h) * HD)
    values = jnp.concatenate([values, jnp.ones_like(values)], axis=1)
    scores = lax.dot_general(
        queries, keys, (((1,), (1,)), ((), ())), preferred_element_type=jnp.float32
    )
    if allowed is not None:
        rows, cols = allowed.shape
        scores = jnp.where(allowed[None], scores.reshape(GROUP, rows, cols), FAR)
        scores = scores.reshape(GROUP * rows, cols)
    parts = lane_groups(scores)
    peak = jnp.max(functools.reduce(jnp.maximum, parts), axis=1, keepdims=True)
    peak = jnp.broadcast_to(peak, parts[0].shape)
    if state is not None:
        peak = jnp.maximum(peak, state[0])
    weights = [jnp.exp2((part - peak) * FACTOR).astype(jnp.bfloat16) for part in parts]
    summed = lax.dot_general(
        jnp.concatenate(weights, axis=1), values, (((1,), (0,)), ((), ())),
        preferred_element_type=jnp.float32,
    )
    if state is not None:
        fade = jnp.exp2((state[0] - peak) * FACTOR)
        summed = summed + state[1] * jnp.concatenate([fade, fade], axis=1)
    return peak, summed


def store_head(h, peak, summed, peak_ref, sum_ref):
    peak_ref[h] = peak
    sum_ref[h] = summed


def finish_head(h, summed, out_ref):
    result = (summed[:, :HD] / summed[:, HD:]).astype(out_ref.dtype)
    rows = out_ref.shape[0]
    for g in range(GROUP):
        at = (h * GROUP + g) * HD
        out_ref[:, at : at + HD] = result[g * rows : (g + 1) * rows]


def own_places(shape, swapped):
    place = lax.rem(lax.axis_index(AXES), PLANE)
    even = lax.rem(place, 2) == 0
    one, two = jnp.where(even, 4, 2), jnp.where(even, 2, 4)
    order = [1, 1 ^ two, 1 ^ one, 7] if swapped else [0, one, two, 6]
    key = lax.broadcasted_iota(jnp.int32, shape, 1)
    return [(place ^ o) * shape[0] + key for o in order]


def may_read(shape, key_places):
    place = lax.rem(lax.axis_index(AXES), PLANE)
    query = place * shape[0] + lax.broadcasted_iota(jnp.int32, shape, 0)
    return jnp.concatenate(key_places, axis=1) <= jnp.concatenate([query] * len(key_places), axis=1)


def own_kernel(q_ref, mine, second, peak_ref, sum_ref):
    shape = (q_ref.shape[0], q_ref.shape[0])
    allowed = may_read(shape, own_places(shape, False))
    for h in range(KVH):
        store_head(h, *fold_head(h, q_ref, (mine, second), allowed, None), peak_ref, sum_ref)


def other_core_kernel(step, q_ref, peak_in, sum_in, *refs):
    blocks, (peak_ref, sum_ref) = refs[:-2], refs[-2:]
    shape = (q_ref.shape[0], q_ref.shape[0])
    group = jnp.full(shape, jnp.where(is_earlier(step), -1, FAR_PLACE), jnp.int32)
    allowed = may_read(shape, own_places(shape, True) + [group] * PLANE)
    for h in range(KVH):
        state = (peak_in[h], sum_in[h])
        store_head(h, *fold_head(h, q_ref, blocks, allowed, state), peak_ref, sum_ref)


def is_earlier(step):
    plane = lax.div(lax.axis_index(AXES), PLANE)
    return (plane ^ step) < plane


def next_kernel(step, q_ref, peak_in, sum_in, *refs):
    blocks, (peak_ref, sum_ref) = refs[:-2], refs[-2:]

    @pl.when(is_earlier(step))
    def _():
        for h in range(KVH):
            state = (peak_in[h], sum_in[h])
            store_head(h, *fold_head(h, q_ref, blocks, None, state), peak_ref, sum_ref)


def last_kernel(step, q_ref, peak_in, sum_in, *refs):
    blocks, out_ref = refs[:-1], refs[-1]
    earlier = is_earlier(step)

    @pl.when(earlier)
    def _():
        for h in range(KVH):
            state = (peak_in[h], sum_in[h])
            finish_head(h, fold_head(h, q_ref, blocks, None, state)[1], out_ref)

    @pl.when(jnp.logical_not(earlier))
    def _():
        for h in range(KVH):
            finish_head(h, sum_in[h], out_ref)


def state_shapes(rows):
    return (
        jax.ShapeDtypeStruct((KVH, GROUP * rows, HD), jnp.float32),
        jax.ShapeDtypeStruct((KVH, GROUP * rows, 2 * HD), jnp.float32),
    )


def call_fold(kernel, name, queries, state, blocks, out_shape, alias):
    operands = [queries, *state, *blocks]
    multi = isinstance(out_shape, tuple)
    return pl.pallas_call(
        kernel,
        out_shape=out_shape,
        in_specs=[VMEM] * len(operands),
        out_specs=(VMEM,) * len(out_shape) if multi else VMEM,
        input_output_aliases={1: 0, 2: 1} if alias else {},
        compiler_params=pltpu.CompilerParams(vmem_limit_bytes=32 * 2**20),
        cost_estimate=FREE,
        name=name,
    )(*operands)


def planes_path(queries, keys, values, count):
    rows = queries.shape[0]
    own = pack(keys, values)

    def exchange(block, even_bits, odd_bits):
        pairs = [(i, i ^ (odd_bits if i % 2 else even_bits)) for i in range(count)]
        return lax.ppermute(block, AXES, pairs)

    def spread(block, join_after=(), swap_after=()):
        mine = join(block, exchange(block, 4, 2), join_after)
        second = exchange(mine, 2, 4)
        return mine, second, exchange(mine, 1, 1), exchange(hold(second, swap_after) if swap_after else second, 1, 1)

    arrived = {1: exchange(own, PLANE, PLANE)}
    arrived[3] = hold(hold(hold(exchange(own, 3 * PLANE, 3 * PLANE))))
    arrived[2] = exchange(arrived[3], PLANE, PLANE)
    mine, second, *swapped = spread(own)
    shapes = state_shapes(rows)
    state = call_fold(own_kernel, "own", queries, (), (mine, second), shapes, False)
    early = (state[0],)
    blocks = (*swapped, *spread(arrived[1]))
    kernel = functools.partial(other_core_kernel, 1)
    state = call_fold(kernel, "other", queries, state, blocks, shapes, True)
    blocks = spread(arrived[3], early)
    kernel = functools.partial(next_kernel, 3)
    state = call_fold(kernel, "next", queries, state, blocks, shapes, True)
    blocks = spread(arrived[2], (), (state[0],))
    out = jax.ShapeDtypeStruct(queries.shape, queries.dtype)
    kernel = functools.partial(last_kernel, 2)
    return call_fold(kernel, "last", queries, state, blocks, out, False)


def span_kernel(pos_ref, q_ref, peak_in, sum_in, kv_ref, peak_ref, sum_ref):
    span, rows = kv_ref.shape[0], q_ref.shape[0]
    first, key_first = pos_ref[0], pos_ref[1] + pl.program_id(0) * span

    @pl.when(pl.program_id(0) == 0)
    def _():
        peak_ref[...] = peak_in[...]
        sum_ref[...] = sum_in[...]

    @pl.when((key_first >= 0) & (key_first < first + rows))
    def _():
        shape = (rows, span)
        key_pos = key_first + lax.broadcasted_iota(jnp.int32, shape, 1)
        allowed = key_pos <= first + lax.broadcasted_iota(jnp.int32, shape, 0)
        for h in range(KVH):
            state = (peak_ref[h], sum_ref[h])
            store_head(h, *fold_head(h, q_ref, (kv_ref,), allowed, state), peak_ref, sum_ref)


def finish_kernel(sum_ref, out_ref):
    for h in range(KVH):
        finish_head(h, sum_ref[h], out_ref)


def ring_path(queries, keys, values, spans):
    rows = queries.shape[0]
    own = pack(keys, values)
    held = lax.all_gather(own, "head", axis=0, tiled=True)
    span_len = held.shape[0]
    span = math.gcd(span_len, 512)
    shapes = state_shapes(rows)
    ctx = lax.axis_index("ctx")
    first = lax.axis_index(AXES) * rows
    whole = [pl.BlockSpec(s.shape, lambda i, d=len(s.shape): (0,) * d) for s in (queries, *shapes)]
    fold = pl.pallas_call(
        span_kernel,
        out_shape=shapes,
        grid=(span_len // span,),
        in_specs=[
            pl.BlockSpec(memory_space=pltpu.SMEM),
            *whole,
            pl.BlockSpec((span, held.shape[1]), lambda i: (i, 0)),
        ],
        out_specs=tuple(whole[1:]),
        compiler_params=pltpu.CompilerParams(vmem_limit_bytes=48 * 2**20),
        name="span",
    )

    def one_step(step, carry):
        held, state = carry
        following = lax.ppermute(held, "ctx", [(i, (i + 1) % spans) for i in range(spans)])
        place = jnp.where(ctx >= step, (ctx - step) * span_len, -span_len)
        state = fold(jnp.stack([first, place]), queries, *state, held)
        return following, tuple(state)

    state = (jnp.full(shapes[0].shape, FAR, jnp.float32), jnp.zeros(shapes[1].shape, jnp.float32))
    sums = lax.fori_loop(0, spans, one_step, (held, state))[1][1]
    return pl.pallas_call(
        finish_kernel,
        out_shape=jax.ShapeDtypeStruct(queries.shape, queries.dtype),
        in_specs=[pl.BlockSpec(memory_space=pltpu.VMEM)],
        out_specs=pl.BlockSpec(memory_space=pltpu.VMEM),
        name="finish",
    )(sums)


def solution(mesh):
    count = mesh.shape["ctx"] * mesh.shape["head"]
    by_planes = mesh.shape["head"] == 4 and mesh.shape["ctx"] == 8

    def shards(queries, keys, values):
        if by_planes:
            return planes_path(queries, keys, values, count)
        return ring_path(queries, keys, values, mesh.shape["ctx"])

    spec = P(AXES, None)
    return jax.shard_map(
        shards, mesh=mesh, in_specs=(spec, spec, spec), out_specs=spec, check_vma=False
    )
```

```python
import functools
import math

import jax
import jax.numpy as jnp
from jax import lax
from jax.experimental import pallas as pl
from jax.experimental.pallas import tpu as pltpu
from jax.sharding import PartitionSpec as P

QH = 32
KVH = 4
HD = 128
GROUP = QH // KVH
AXES = ("ctx", "head")
PLANE = 8
FAR = -1e30
FACTOR = math.log2(math.e) / math.sqrt(HD)
VMEM = pl.BlockSpec(memory_space=pltpu.VMEM)
FREE = pl.CostEstimate(flops=0, bytes_accessed=0, transcendentals=0)


def pack_kernel(keys_ref, values_ref, out_ref, sems):
    width = keys_ref.shape[1]
    copies = [
        pltpu.make_async_copy(keys_ref, out_ref.at[:, :width], sems.at[0]),
        pltpu.make_async_copy(values_ref, out_ref.at[:, width:], sems.at[1]),
    ]
    for copy in copies:
        copy.start()
    for copy in copies:
        copy.wait()


def pack(keys, values):
    rows, width = keys.shape
    return pl.pallas_call(
        pack_kernel,
        out_shape=jax.ShapeDtypeStruct((rows, 2 * width), keys.dtype),
        in_specs=[pl.BlockSpec(memory_space=pltpu.HBM)] * 2,
        out_specs=VMEM,
        scratch_shapes=[pltpu.SemaphoreType.DMA((2,))],
        compiler_params=pltpu.CompilerParams(vmem_limit_bytes=2 * 2**20),
        name="pack",
    )(keys, values)


def join_kernel(count, *refs):
    out_ref, rows = refs[-1], 0
    for ref in refs[:count]:
        out_ref[rows : rows + ref.shape[0]] = ref[...]
        rows += ref.shape[0]


def move(kernel, name, blocks, rows, after=()):
    return pl.pallas_call(
        kernel,
        out_shape=jax.ShapeDtypeStruct((rows, blocks[0].shape[1]), blocks[0].dtype),
        in_specs=[VMEM] * len(blocks) + [pl.BlockSpec(memory_space=pl.ANY)] * len(after),
        out_specs=VMEM,
        compiler_params=pltpu.CompilerParams(vmem_limit_bytes=2 * 2**20),
        cost_estimate=FREE,
        name=name,
    )(*blocks, *after)


def join(*blocks, after=()):
    kernel = functools.partial(join_kernel, len(blocks))
    return move(kernel, "join", blocks, sum(b.shape[0] for b in blocks), after)


def hold(block, times=1, after=()):
    for _ in range(times):
        block = join(block, after=after)
    return block


def columns(blocks, at):
    return jnp.concatenate([b[:, at : at + HD] for b in blocks], axis=0)


def weigh(scores, spec, marks):
    if spec[0] == "step":
        return scores + marks[spec]
    rows, cols = marks[spec].shape
    scores = jnp.where(marks[spec][None], scores.reshape(GROUP, rows, cols), FAR)
    return scores.reshape(GROUP * rows, cols)


def make_marks(specs, rows):
    index = lax.axis_index(AXES)
    place, plane = lax.rem(index, PLANE), lax.div(index, PLANE)
    even = lax.rem(place, 2) == 0
    one, two = jnp.where(even, 4, 2), jnp.where(even, 2, 4)
    orders = {"mine": (0, one), "second": (two, 6), "mine_": (1, 1 ^ two), "second_": (1 ^ one, 7)}
    shape = (rows, rows)
    query = place * rows + lax.broadcasted_iota(jnp.int32, shape, 0)
    query = jnp.concatenate([query, query], axis=1)
    key = lax.broadcasted_iota(jnp.int32, shape, 1)
    marks = {}
    for spec in specs:
        if spec[0] == "step":
            marks[spec] = jnp.where((plane ^ spec[1]) < plane, 0.0, FAR)
        else:
            places = [(place ^ o) * rows + key for o in orders[spec[1]]]
            marks[spec] = jnp.concatenate(places, axis=1) <= query
    return marks


def fold_head(h, q_ref, blocks, specs, marks, state):
    queries = jnp.concatenate(
        [q_ref[:, (h * GROUP + g) * HD : (h * GROUP + g + 1) * HD] for g in range(GROUP)], axis=0
    )
    keys = columns(blocks, h * HD)
    values = columns(blocks, (KVH + h) * HD)
    values = jnp.concatenate([values, jnp.ones_like(values)], axis=1)
    scores = lax.dot_general(
        queries, keys, (((1,), (1,)), ((), ())), preferred_element_type=jnp.float32
    )
    parts = [scores[:, at : at + HD] for at in range(0, scores.shape[1], HD)]
    parts = [weigh(part, spec, marks) for part, spec in zip(parts, specs, strict=True)]
    peak = jnp.max(functools.reduce(jnp.maximum, parts), axis=1, keepdims=True)
    peak = jnp.broadcast_to(peak, parts[0].shape)
    if state is not None:
        peak = jnp.maximum(peak, state[0])
    weights = [jnp.exp2((part - peak) * FACTOR).astype(jnp.bfloat16) for part in parts]
    summed = lax.dot_general(
        jnp.concatenate(weights, axis=1), values, (((1,), (0,)), ((), ())),
        preferred_element_type=jnp.float32,
    )
    if state is not None:
        fade = jnp.exp2((state[0] - peak) * FACTOR)
        summed = summed + state[1] * jnp.concatenate([fade, fade], axis=1)
    return peak, summed


def finish_head(h, summed, out_ref):
    result = (summed[:, :HD] / summed[:, HD:]).astype(out_ref.dtype)
    rows = out_ref.shape[0]
    for g in range(GROUP):
        at = (h * GROUP + g) * HD
        out_ref[:, at : at + HD] = result[g * rows : (g + 1) * rows]


def fold_kernel(specs, has_state, last, q_ref, *refs):
    state_refs, refs = (refs[:2], refs[2:]) if has_state else ((), refs)
    blocks, outs = (refs[:-1], refs[-1:]) if last else (refs[:-2], refs[-2:])
    marks = make_marks(specs, q_ref.shape[0])
    for h in range(KVH):
        state = tuple(ref[h] for ref in state_refs) or None
        peak, summed = fold_head(h, q_ref, blocks, specs, marks, state)
        if last:
            finish_head(h, summed, outs[0])
        else:
            outs[0][h], outs[1][h] = peak, summed


def state_shapes(rows):
    return (
        jax.ShapeDtypeStruct((KVH, GROUP * rows, HD), jnp.float32),
        jax.ShapeDtypeStruct((KVH, GROUP * rows, 2 * HD), jnp.float32),
    )


def fold(queries, state, pieces, last=False):
    rows = queries.shape[0]
    blocks = [block for block, _ in pieces]
    specs = tuple(spec for _, block_specs in pieces for spec in block_specs)
    operands = [queries, *state, *blocks]
    out_shape = jax.ShapeDtypeStruct(queries.shape, queries.dtype) if last else state_shapes(rows)
    return pl.pallas_call(
        functools.partial(fold_kernel, specs, bool(state), last),
        out_shape=out_shape,
        in_specs=[VMEM] * len(operands),
        out_specs=VMEM if last else (VMEM, VMEM),
        input_output_aliases={1: 0, 2: 1} if state and not last else {},
        compiler_params=pltpu.CompilerParams(vmem_limit_bytes=32 * 2**20),
        cost_estimate=FREE,
        name=f"fold{len(specs)}{'s' if state else 'n'}{'l' if last else ''}",
    )(*operands)


def planes_path(queries, keys, values, count):
    rows = queries.shape[0]
    own = pack(keys, values)

    def exchange(block, even_bits, odd_bits):
        pairs = [(i, i ^ (odd_bits if i % 2 else even_bits)) for i in range(count)]
        return lax.ppermute(block, AXES, pairs)

    def swap(block):
        return exchange(block, 1, 1)

    def double(block, after=()):
        mine = join(block, exchange(block, 4, 2), after=after)
        return mine, exchange(mine, 2, 4)

    group3 = hold(exchange(own, 3 * PLANE, 3 * PLANE), 3)
    group2 = hold(exchange(group3, PLANE, PLANE), 1)
    mine_own, second_own = ("own", "mine"), ("own", "second")
    mine_swapped, second_swapped = ("own", "mine_"), ("own", "second_")
    mine0, second0 = double(own)
    swapped0 = (swap(mine0), swap(second0))
    state = fold(queries, (), [(mine0, (mine_own,)), (second0, (second_own,))])
    early = (state[0],)
    mine1, second1 = hold(exchange(mine0, PLANE, PLANE), 1), exchange(second0, PLANE, PLANE)
    swapped1 = (swap(mine1), swap(second1))
    state = fold(queries, state, [(swapped0[0], (mine_swapped,)), (swapped0[1], (second_swapped,)), (mine1, (("step", 1),)), (second1, (("step", 1),)), (swapped1[0], (("step", 1),)), (swapped1[1], (("step", 1),))])
    mine3, second3 = double(group3)
    mine2, second2 = double(group2, after=early)
    swapped3 = (swap(mine3), swap(second3))
    state = fold(queries, state, [(mine3, (("step", 3),)), (second3, (("step", 3),)), (swapped3[0], (("step", 3),)), (swapped3[1], (("step", 3),))])
    swapped2 = (swap(mine2), swap(hold(second2, after=(state[0],))))
    pieces = [(mine2, (("step", 2),)), (second2, (("step", 2),)), (swapped2[0], (("step", 2),)), (swapped2[1], (("step", 2),))]
    return fold(queries, state, pieces, last=True)


def span_kernel(pos_ref, q_ref, peak_in, sum_in, kv_ref, peak_ref, sum_ref):
    span, rows = kv_ref.shape[0], q_ref.shape[0]
    first, key_first = pos_ref[0], pos_ref[1] + pl.program_id(0) * span

    @pl.when(pl.program_id(0) == 0)
    def _():
        peak_ref[...] = peak_in[...]
        sum_ref[...] = sum_in[...]

    @pl.when((key_first >= 0) & (key_first < first + rows))
    def _():
        shape = (rows, span)
        key_pos = key_first + lax.broadcasted_iota(jnp.int32, shape, 1)
        allowed = key_pos <= first + lax.broadcasted_iota(jnp.int32, shape, 0)
        specs = [("key", at) for at in range(0, span, HD)]
        marks = {spec: allowed[:, spec[1] : spec[1] + HD] for spec in specs}
        for h in range(KVH):
            state = (peak_ref[h], sum_ref[h])
            peak_ref[h], sum_ref[h] = fold_head(h, q_ref, (kv_ref,), specs, marks, state)


def finish_kernel(sum_ref, out_ref):
    for h in range(KVH):
        finish_head(h, sum_ref[h], out_ref)


def ring_path(queries, keys, values, spans):
    rows = queries.shape[0]
    own = pack(keys, values)
    held = lax.all_gather(own, "head", axis=0, tiled=True)
    span_len = held.shape[0]
    span = math.gcd(span_len, 512)
    shapes = state_shapes(rows)
    ctx = lax.axis_index("ctx")
    first = lax.axis_index(AXES) * rows
    whole = [pl.BlockSpec(s.shape, lambda i, d=len(s.shape): (0,) * d) for s in (queries, *shapes)]
    fold = pl.pallas_call(
        span_kernel,
        out_shape=shapes,
        grid=(span_len // span,),
        in_specs=[
            pl.BlockSpec(memory_space=pltpu.SMEM),
            *whole,
            pl.BlockSpec((span, held.shape[1]), lambda i: (i, 0)),
        ],
        out_specs=tuple(whole[1:]),
        compiler_params=pltpu.CompilerParams(vmem_limit_bytes=48 * 2**20),
        name="span",
    )

    def one_step(step, carry):
        held, state = carry
        following = lax.ppermute(held, "ctx", [(i, (i + 1) % spans) for i in range(spans)])
        place = jnp.where(ctx >= step, (ctx - step) * span_len, -span_len)
        state = fold(jnp.stack([first, place]), queries, *state, held)
        return following, tuple(state)

    state = (jnp.full(shapes[0].shape, FAR, jnp.float32), jnp.zeros(shapes[1].shape, jnp.float32))
    sums = lax.fori_loop(0, spans, one_step, (held, state))[1][1]
    return pl.pallas_call(
        finish_kernel,
        out_shape=jax.ShapeDtypeStruct(queries.shape, queries.dtype),
        in_specs=[pl.BlockSpec(memory_space=pltpu.VMEM)],
        out_specs=pl.BlockSpec(memory_space=pltpu.VMEM),
        name="finish",
    )(sums)


def solution(mesh):
    count = mesh.shape["ctx"] * mesh.shape["head"]
    by_planes = mesh.shape["head"] == 4 and mesh.shape["ctx"] == 8

    def shards(queries, keys, values):
        if by_planes:
            return planes_path(queries, keys, values, count)
        return ring_path(queries, keys, values, mesh.shape["ctx"])

    spec = P(AXES, None)
    return jax.shard_map(
        shards, mesh=mesh, in_specs=(spec, spec, spec), out_specs=spec, check_vma=False
    )
```

```python
import functools
import math

import jax
import jax.numpy as jnp
from jax import lax
from jax.experimental import pallas as pl
from jax.experimental.pallas import tpu as pltpu
from jax.sharding import PartitionSpec as P

QH = 32
KVH = 4
HD = 128
GROUP = QH // KVH
AXES = ("ctx", "head")
PLANE = 8
FAR = -1e30
FACTOR = math.log2(math.e) / math.sqrt(HD)
VMEM = pl.BlockSpec(memory_space=pltpu.VMEM)
FREE = pl.CostEstimate(flops=0, bytes_accessed=0, transcendentals=0)


def pack_kernel(keys_ref, values_ref, out_ref, sems):
    width = keys_ref.shape[1]
    copies = [
        pltpu.make_async_copy(keys_ref, out_ref.at[:, :width], sems.at[0]),
        pltpu.make_async_copy(values_ref, out_ref.at[:, width:], sems.at[1]),
    ]
    for copy in copies:
        copy.start()
    for copy in copies:
        copy.wait()


def pack(keys, values):
    rows, width = keys.shape
    return pl.pallas_call(
        pack_kernel,
        out_shape=jax.ShapeDtypeStruct((rows, 2 * width), keys.dtype),
        in_specs=[pl.BlockSpec(memory_space=pltpu.HBM)] * 2,
        out_specs=VMEM,
        scratch_shapes=[pltpu.SemaphoreType.DMA((2,))],
        compiler_params=pltpu.CompilerParams(vmem_limit_bytes=2 * 2**20),
        name="pack",
    )(keys, values)


def join_kernel(count, *refs):
    out_ref, rows = refs[-1], 0
    for ref in refs[:count]:
        out_ref[rows : rows + ref.shape[0]] = ref[...]
        rows += ref.shape[0]


def move(kernel, name, blocks, rows, after=()):
    return pl.pallas_call(
        kernel,
        out_shape=jax.ShapeDtypeStruct((rows, blocks[0].shape[1]), blocks[0].dtype),
        in_specs=[VMEM] * len(blocks) + [pl.BlockSpec(memory_space=pl.ANY)] * len(after),
        out_specs=VMEM,
        compiler_params=pltpu.CompilerParams(vmem_limit_bytes=2 * 2**20),
        cost_estimate=FREE,
        name=name,
    )(*blocks, *after)


def join(*blocks, after=()):
    kernel = functools.partial(join_kernel, len(blocks))
    return move(kernel, "join", blocks, sum(b.shape[0] for b in blocks), after)


def hold(block, times=1, after=()):
    for _ in range(times):
        block = join(block, after=after)
    return block


def columns(blocks, at):
    return jnp.concatenate([b[:, at : at + HD] for b in blocks], axis=0)


def weigh(scores, spec, marks):
    if spec not in marks:
        return scores
    if spec[0] == "step":
        return scores + marks[spec]
    rows, cols = marks[spec].shape
    scores = jnp.where(marks[spec][None], scores.reshape(GROUP, rows, cols), FAR)
    return scores.reshape(GROUP * rows, cols)


def make_marks(specs, rows):
    index = lax.axis_index(AXES)
    place, plane = lax.rem(index, PLANE), lax.div(index, PLANE)
    even = lax.rem(place, 2) == 0
    one, two = jnp.where(even, 4, 2), jnp.where(even, 2, 4)
    orders = {"mine": (0, one), "second": (two, 6), "mine_": (1, 1 ^ two), "second_": (1 ^ one, 7)}
    shape = (rows, rows)
    query = place * rows + lax.broadcasted_iota(jnp.int32, shape, 0)
    query = jnp.concatenate([query, query], axis=1)
    key = lax.broadcasted_iota(jnp.int32, shape, 1)
    marks = {}
    for spec in specs:
        if spec[0] == "step":
            marks[spec] = jnp.where((plane ^ spec[1]) < plane, 0.0, FAR)
        else:
            places = [(place ^ o) * rows + key for o in orders[spec[1]]]
            marks[spec] = jnp.concatenate(places, axis=1) <= query
    return marks


def fold_head(h, q_ref, blocks, specs, marks, state):
    queries = jnp.concatenate(
        [q_ref[:, (h * GROUP + g) * HD : (h * GROUP + g + 1) * HD] for g in range(GROUP)], axis=0
    )
    keys = columns(blocks, h * HD)
    values = columns(blocks, (KVH + h) * HD)
    values = jnp.concatenate([values, jnp.ones_like(values)], axis=1)
    scores = lax.dot_general(
        queries, keys, (((1,), (1,)), ((), ())), preferred_element_type=jnp.float32
    )
    parts = [scores[:, at : at + HD] for at in range(0, scores.shape[1], HD)]
    parts = [weigh(part, spec, marks) for part, spec in zip(parts, specs, strict=True)]
    peak = jnp.max(functools.reduce(jnp.maximum, parts), axis=1, keepdims=True)
    peak = jnp.broadcast_to(peak, parts[0].shape)
    if state is not None:
        peak = jnp.maximum(peak, state[0])
    weights = [jnp.exp2((part - peak) * FACTOR).astype(jnp.bfloat16) for part in parts]
    summed = lax.dot_general(
        jnp.concatenate(weights, axis=1), values, (((1,), (0,)), ((), ())),
        preferred_element_type=jnp.float32,
    )
    if state is not None:
        fade = jnp.exp2((state[0] - peak) * FACTOR)
        summed = summed + state[1] * jnp.concatenate([fade, fade], axis=1)
    return peak, summed


def finish_head(h, summed, out_ref):
    result = (summed[:, :HD] / summed[:, HD:]).astype(out_ref.dtype)
    rows = out_ref.shape[0]
    for g in range(GROUP):
        at = (h * GROUP + g) * HD
        out_ref[:, at : at + HD] = result[g * rows : (g + 1) * rows]


def fold_kernel(specs, has_state, last, q_ref, *refs):
    state_refs, refs = (refs[:2], refs[2:]) if has_state else ((), refs)
    blocks, outs = (refs[:-1], refs[-1:]) if last else (refs[:-2], refs[-2:])
    marks = make_marks(specs, q_ref.shape[0])
    steps = {spec for spec in specs if spec[0] == "step"}
    single = len(steps) == 1 and steps == set(specs) and has_state

    def work():
        for h in range(KVH):
            state = tuple(ref[h] for ref in state_refs) or None
            peak, summed = fold_head(h, q_ref, blocks, specs, {} if single else marks, state)
            if last:
                finish_head(h, summed, outs[0])
            else:
                outs[0][h], outs[1][h] = peak, summed

    if not single:
        work()
        return
    valid = marks[specs[0]] == 0.0
    pl.when(valid)(work)
    if last:

        @pl.when(jnp.logical_not(valid))
        def _():
            for h in range(KVH):
                finish_head(h, state_refs[1][h], outs[0])


def state_shapes(rows):
    return (
        jax.ShapeDtypeStruct((KVH, GROUP * rows, HD), jnp.float32),
        jax.ShapeDtypeStruct((KVH, GROUP * rows, 2 * HD), jnp.float32),
    )


def fold(queries, state, pieces, last=False):
    rows = queries.shape[0]
    blocks = [block for block, _ in pieces]
    specs = tuple(spec for _, block_specs in pieces for spec in block_specs)
    operands = [queries, *state, *blocks]
    out_shape = jax.ShapeDtypeStruct(queries.shape, queries.dtype) if last else state_shapes(rows)
    return pl.pallas_call(
        functools.partial(fold_kernel, specs, bool(state), last),
        out_shape=out_shape,
        in_specs=[VMEM] * len(operands),
        out_specs=VMEM if last else (VMEM, VMEM),
        input_output_aliases={1: 0, 2: 1} if state and not last else {},
        compiler_params=pltpu.CompilerParams(vmem_limit_bytes=32 * 2**20),
        cost_estimate=FREE,
        name=f"fold{len(specs)}{'s' if state else 'n'}{'l' if last else ''}",
    )(*operands)


def planes_path(queries, keys, values, count):
    rows = queries.shape[0]
    own = pack(keys, values)

    def exchange(block, even_bits, odd_bits):
        pairs = [(i, i ^ (odd_bits if i % 2 else even_bits)) for i in range(count)]
        return lax.ppermute(block, AXES, pairs)

    def swap(block):
        return exchange(block, 1, 1)

    def double(block, after=()):
        mine = join(block, exchange(block, 4, 2), after=after)
        return mine, exchange(mine, 2, 4)

    group3 = hold(exchange(own, 3 * PLANE, 3 * PLANE), 3)
    group2 = hold(exchange(group3, PLANE, PLANE))
    of_own = (("own", "mine"),), (("own", "second"),), (("own", "mine_"),), (("own", "second_"),)
    of_1, of_2, of_3 = ((("step", step),) for step in (1, 2, 3))

    mine0, second0 = double(own)
    swapped0 = [swap(mine0), swap(second0)]
    state = fold(queries, (), list(zip([mine0, second0], of_own)))
    early = (state[0],)

    mine1, second1 = hold(exchange(mine0, PLANE, PLANE)), exchange(second0, PLANE, PLANE)
    mine3, second3 = double(group3)
    from1 = [mine1, second1, swap(mine1), swap(second1)]
    from3 = [mine3, second3, swap(mine3), swap(second3)]
    state = fold(queries, state, list(zip(swapped0 + from1, [*of_own[2:], *[of_1] * 4])))
    state = fold(queries, state, list(zip(from3, [of_3] * 4)))

    mine2, second2 = double(group2, after=early)
    pieces = [mine2, second2, swap(mine2), swap(hold(second2, after=(state[0],)))]
    return fold(queries, state, [(piece, of_2) for piece in pieces], last=True)


def span_kernel(pos_ref, q_ref, peak_in, sum_in, kv_ref, peak_ref, sum_ref):
    span, rows = kv_ref.shape[0], q_ref.shape[0]
    first, key_first = pos_ref[0], pos_ref[1] + pl.program_id(0) * span

    @pl.when(pl.program_id(0) == 0)
    def _():
        peak_ref[...] = peak_in[...]
        sum_ref[...] = sum_in[...]

    @pl.when((key_first >= 0) & (key_first < first + rows))
    def _():
        shape = (rows, span)
        key_pos = key_first + lax.broadcasted_iota(jnp.int32, shape, 1)
        allowed = key_pos <= first + lax.broadcasted_iota(jnp.int32, shape, 0)
        specs = [("key", at) for at in range(0, span, HD)]
        marks = {spec: allowed[:, spec[1] : spec[1] + HD] for spec in specs}
        for h in range(KVH):
            state = (peak_ref[h], sum_ref[h])
            peak_ref[h], sum_ref[h] = fold_head(h, q_ref, (kv_ref,), specs, marks, state)


def finish_kernel(sum_ref, out_ref):
    for h in range(KVH):
        finish_head(h, sum_ref[h], out_ref)


def ring_path(queries, keys, values, spans):
    rows = queries.shape[0]
    own = pack(keys, values)
    held = lax.all_gather(own, "head", axis=0, tiled=True)
    span_len = held.shape[0]
    span = math.gcd(span_len, 512)
    shapes = state_shapes(rows)
    ctx = lax.axis_index("ctx")
    first = lax.axis_index(AXES) * rows
    whole = [pl.BlockSpec(s.shape, lambda i, d=len(s.shape): (0,) * d) for s in (queries, *shapes)]
    fold = pl.pallas_call(
        span_kernel,
        out_shape=shapes,
        grid=(span_len // span,),
        in_specs=[
            pl.BlockSpec(memory_space=pltpu.SMEM),
            *whole,
            pl.BlockSpec((span, held.shape[1]), lambda i: (i, 0)),
        ],
        out_specs=tuple(whole[1:]),
        compiler_params=pltpu.CompilerParams(vmem_limit_bytes=48 * 2**20),
        name="span",
    )

    def one_step(step, carry):
        held, state = carry
        following = lax.ppermute(held, "ctx", [(i, (i + 1) % spans) for i in range(spans)])
        place = jnp.where(ctx >= step, (ctx - step) * span_len, -span_len)
        state = fold(jnp.stack([first, place]), queries, *state, held)
        return following, tuple(state)

    state = (jnp.full(shapes[0].shape, FAR, jnp.float32), jnp.zeros(shapes[1].shape, jnp.float32))
    sums = lax.fori_loop(0, spans, one_step, (held, state))[1][1]
    return pl.pallas_call(
        finish_kernel,
        out_shape=jax.ShapeDtypeStruct(queries.shape, queries.dtype),
        in_specs=[pl.BlockSpec(memory_space=pltpu.VMEM)],
        out_specs=pl.BlockSpec(memory_space=pltpu.VMEM),
        name="finish",
    )(sums)


def solution(mesh):
    count = mesh.shape["ctx"] * mesh.shape["head"]
    by_planes = mesh.shape["head"] == 4 and mesh.shape["ctx"] == 8

    def shards(queries, keys, values):
        if by_planes:
            return planes_path(queries, keys, values, count)
        return ring_path(queries, keys, values, mesh.shape["ctx"])

    spec = P(AXES, None)
    return jax.shard_map(
        shards, mesh=mesh, in_specs=(spec, spec, spec), out_specs=spec, check_vma=False
    )
```

```python
import functools
import math

import jax
import jax.numpy as jnp
from jax import lax
from jax.experimental import pallas as pl
from jax.experimental.pallas import tpu as pltpu
from jax.sharding import PartitionSpec as P

QH = 32
KVH = 4
HD = 128
GROUP = QH // KVH
AXES = ("ctx", "head")
PLANE = 8
FAR = -1e30
FACTOR = math.log2(math.e) / math.sqrt(HD)
VMEM = pl.BlockSpec(memory_space=pltpu.VMEM)
FREE = pl.CostEstimate(flops=0, bytes_accessed=0, transcendentals=0)


def pack_kernel(keys_ref, values_ref, out_ref, sems):
    width = keys_ref.shape[1]
    copies = [
        pltpu.make_async_copy(keys_ref, out_ref.at[:, :width], sems.at[0]),
        pltpu.make_async_copy(values_ref, out_ref.at[:, width:], sems.at[1]),
    ]
    for copy in copies:
        copy.start()
    for copy in copies:
        copy.wait()


def pack(keys, values):
    rows, width = keys.shape
    return pl.pallas_call(
        pack_kernel,
        out_shape=jax.ShapeDtypeStruct((rows, 2 * width), keys.dtype),
        in_specs=[pl.BlockSpec(memory_space=pltpu.HBM)] * 2,
        out_specs=VMEM,
        scratch_shapes=[pltpu.SemaphoreType.DMA((2,))],
        compiler_params=pltpu.CompilerParams(vmem_limit_bytes=2 * 2**20),
        name="pack",
    )(keys, values)


def join_kernel(count, *refs):
    out_ref, rows = refs[-1], 0
    for ref in refs[:count]:
        out_ref[rows : rows + ref.shape[0]] = ref[...]
        rows += ref.shape[0]


def move(kernel, name, blocks, rows, after=()):
    return pl.pallas_call(
        kernel,
        out_shape=jax.ShapeDtypeStruct((rows, blocks[0].shape[1]), blocks[0].dtype),
        in_specs=[VMEM] * len(blocks) + [pl.BlockSpec(memory_space=pl.ANY)] * len(after),
        out_specs=VMEM,
        compiler_params=pltpu.CompilerParams(vmem_limit_bytes=2 * 2**20),
        cost_estimate=FREE,
        name=name,
    )(*blocks, *after)


def join(*blocks, after=()):
    kernel = functools.partial(join_kernel, len(blocks))
    return move(kernel, "join", blocks, sum(b.shape[0] for b in blocks), after)


def hold(block, times=1, after=()):
    for _ in range(times):
        block = join(block, after=after)
    return block


def columns(blocks, at):
    return jnp.concatenate([b[:, at : at + HD] for b in blocks], axis=0)


def weigh(scores, spec, marks):
    if spec not in marks:
        return scores
    if spec[0] == "step":
        return scores + marks[spec]
    rows, cols = marks[spec].shape
    scores = jnp.where(marks[spec][None], scores.reshape(GROUP, rows, cols), FAR)
    return scores.reshape(GROUP * rows, cols)


def make_marks(specs, rows):
    index = lax.axis_index(AXES)
    place, plane = lax.rem(index, PLANE), lax.div(index, PLANE)
    even = lax.rem(place, 2) == 0
    one, two = jnp.where(even, 4, 2), jnp.where(even, 2, 4)
    orders = {"mine": (0, one), "second": (two, 6), "mine_": (1, 1 ^ two), "second_": (1 ^ one, 7)}
    shape = (rows, rows)
    query = place * rows + lax.broadcasted_iota(jnp.int32, shape, 0)
    query = jnp.concatenate([query, query], axis=1)
    key = lax.broadcasted_iota(jnp.int32, shape, 1)
    marks = {}
    for spec in specs:
        if spec[0] == "step":
            marks[spec] = jnp.where((plane ^ spec[1]) < plane, 0.0, FAR)
        else:
            places = [(place ^ o) * rows + key for o in orders[spec[1]]]
            marks[spec] = jnp.concatenate(places, axis=1) <= query
    return marks


def fold_head(h, q_ref, blocks, specs, marks, state):
    queries = jnp.concatenate(
        [q_ref[:, (h * GROUP + g) * HD : (h * GROUP + g + 1) * HD] for g in range(GROUP)], axis=0
    )
    keys = columns(blocks, h * HD)
    values = columns(blocks, (KVH + h) * HD)
    values = jnp.concatenate([values, jnp.ones_like(values)], axis=1)
    scores = lax.dot_general(
        queries, keys, (((1,), (1,)), ((), ())), preferred_element_type=jnp.float32
    )
    parts = [scores[:, at : at + HD] for at in range(0, scores.shape[1], HD)]
    parts = [weigh(part, spec, marks) for part, spec in zip(parts, specs, strict=True)]
    peak = jnp.max(functools.reduce(jnp.maximum, parts), axis=1, keepdims=True)
    peak = jnp.broadcast_to(peak, parts[0].shape)
    if state is not None:
        peak = jnp.maximum(peak, state[0])
    weights = [jnp.exp2(((part - peak) * FACTOR).astype(jnp.bfloat16)) for part in parts]
    summed = lax.dot_general(
        jnp.concatenate(weights, axis=1), values, (((1,), (0,)), ((), ())),
        preferred_element_type=jnp.float32,
    )
    if state is not None:
        fade = jnp.exp2((state[0] - peak) * FACTOR)
        summed = summed + state[1] * jnp.concatenate([fade, fade], axis=1)
    return peak, summed


def finish_head(h, summed, out_ref):
    result = (summed[:, :HD] / summed[:, HD:]).astype(out_ref.dtype)
    rows = out_ref.shape[0]
    for g in range(GROUP):
        at = (h * GROUP + g) * HD
        out_ref[:, at : at + HD] = result[g * rows : (g + 1) * rows]


def fold_kernel(specs, has_state, last, q_ref, *refs):
    state_refs, refs = (refs[:2], refs[2:]) if has_state else ((), refs)
    blocks, outs = (refs[:-1], refs[-1:]) if last else (refs[:-2], refs[-2:])
    marks = make_marks(specs, q_ref.shape[0])
    steps = {spec for spec in specs if spec[0] == "step"}
    single = len(steps) == 1 and steps == set(specs) and has_state

    def work():
        for h in range(KVH):
            state = tuple(ref[h] for ref in state_refs) or None
            peak, summed = fold_head(h, q_ref, blocks, specs, {} if single else marks, state)
            if last:
                finish_head(h, summed, outs[0])
            else:
                outs[0][h], outs[1][h] = peak, summed

    if not single:
        work()
        return
    valid = marks[specs[0]] == 0.0
    pl.when(valid)(work)
    if last:

        @pl.when(jnp.logical_not(valid))
        def _():
            for h in range(KVH):
                finish_head(h, state_refs[1][h], outs[0])


def state_shapes(rows):
    return (
        jax.ShapeDtypeStruct((KVH, GROUP * rows, HD), jnp.float32),
        jax.ShapeDtypeStruct((KVH, GROUP * rows, 2 * HD), jnp.float32),
    )


def fold(queries, state, pieces, last=False):
    rows = queries.shape[0]
    blocks = [block for block, _ in pieces]
    specs = tuple(spec for _, block_specs in pieces for spec in block_specs)
    operands = [queries, *state, *blocks]
    out_shape = jax.ShapeDtypeStruct(queries.shape, queries.dtype) if last else state_shapes(rows)
    return pl.pallas_call(
        functools.partial(fold_kernel, specs, bool(state), last),
        out_shape=out_shape,
        in_specs=[VMEM] * len(operands),
        out_specs=VMEM if last else (VMEM, VMEM),
        input_output_aliases={1: 0, 2: 1} if state and not last else {},
        compiler_params=pltpu.CompilerParams(vmem_limit_bytes=32 * 2**20),
        cost_estimate=FREE,
        name=f"fold{len(specs)}{'s' if state else 'n'}{'l' if last else ''}",
    )(*operands)


def planes_path(queries, keys, values, count):
    rows = queries.shape[0]
    own = pack(keys, values)

    def exchange(block, even_bits, odd_bits):
        pairs = [(i, i ^ (odd_bits if i % 2 else even_bits)) for i in range(count)]
        return lax.ppermute(block, AXES, pairs)

    def swap(block):
        return exchange(block, 1, 1)

    def double(block, after=()):
        mine = join(block, exchange(block, 4, 2), after=after)
        return mine, exchange(mine, 2, 4)

    group3 = hold(exchange(own, 3 * PLANE, 3 * PLANE), 3)
    group2 = hold(exchange(group3, PLANE, PLANE))
    of_own = (("own", "mine"),), (("own", "second"),), (("own", "mine_"),), (("own", "second_"),)
    of_1, of_2, of_3 = ((("step", step),) for step in (1, 2, 3))

    mine0, second0 = double(own)
    swapped0 = [swap(mine0), swap(second0)]
    state = fold(queries, (), list(zip([mine0, second0], of_own)))
    early = (state[0],)

    mine1, second1 = hold(exchange(mine0, PLANE, PLANE)), exchange(second0, PLANE, PLANE)
    mine3, second3 = double(group3)
    from1 = [mine1, second1, swap(mine1), swap(second1)]
    from3 = [mine3, second3, swap(mine3), swap(second3)]
    state = fold(queries, state, list(zip(swapped0 + from1, [*of_own[2:], *[of_1] * 4])))
    state = fold(queries, state, list(zip(from3, [of_3] * 4)))

    mine2, second2 = double(group2, after=early)
    pieces = [mine2, second2, swap(mine2), swap(hold(second2, after=(state[0],)))]
    return fold(queries, state, [(piece, of_2) for piece in pieces], last=True)


def span_kernel(pos_ref, q_ref, peak_in, sum_in, kv_ref, peak_ref, sum_ref):
    span, rows = kv_ref.shape[0], q_ref.shape[0]
    first, key_first = pos_ref[0], pos_ref[1] + pl.program_id(0) * span

    @pl.when(pl.program_id(0) == 0)
    def _():
        peak_ref[...] = peak_in[...]
        sum_ref[...] = sum_in[...]

    @pl.when((key_first >= 0) & (key_first < first + rows))
    def _():
        shape = (rows, span)
        key_pos = key_first + lax.broadcasted_iota(jnp.int32, shape, 1)
        allowed = key_pos <= first + lax.broadcasted_iota(jnp.int32, shape, 0)
        specs = [("key", at) for at in range(0, span, HD)]
        marks = {spec: allowed[:, spec[1] : spec[1] + HD] for spec in specs}
        for h in range(KVH):
            state = (peak_ref[h], sum_ref[h])
            peak_ref[h], sum_ref[h] = fold_head(h, q_ref, (kv_ref,), specs, marks, state)


def finish_kernel(sum_ref, out_ref):
    for h in range(KVH):
        finish_head(h, sum_ref[h], out_ref)


def ring_path(queries, keys, values, spans):
    rows = queries.shape[0]
    own = pack(keys, values)
    held = lax.all_gather(own, "head", axis=0, tiled=True)
    span_len = held.shape[0]
    span = math.gcd(span_len, 512)
    shapes = state_shapes(rows)
    ctx = lax.axis_index("ctx")
    first = lax.axis_index(AXES) * rows
    whole = [pl.BlockSpec(s.shape, lambda i, d=len(s.shape): (0,) * d) for s in (queries, *shapes)]
    fold = pl.pallas_call(
        span_kernel,
        out_shape=shapes,
        grid=(span_len // span,),
        in_specs=[
            pl.BlockSpec(memory_space=pltpu.SMEM),
            *whole,
            pl.BlockSpec((span, held.shape[1]), lambda i: (i, 0)),
        ],
        out_specs=tuple(whole[1:]),
        compiler_params=pltpu.CompilerParams(vmem_limit_bytes=48 * 2**20),
        name="span",
    )

    def one_step(step, carry):
        held, state = carry
        following = lax.ppermute(held, "ctx", [(i, (i + 1) % spans) for i in range(spans)])
        place = jnp.where(ctx >= step, (ctx - step) * span_len, -span_len)
        state = fold(jnp.stack([first, place]), queries, *state, held)
        return following, tuple(state)

    state = (jnp.full(shapes[0].shape, FAR, jnp.float32), jnp.zeros(shapes[1].shape, jnp.float32))
    sums = lax.fori_loop(0, spans, one_step, (held, state))[1][1]
    return pl.pallas_call(
        finish_kernel,
        out_shape=jax.ShapeDtypeStruct(queries.shape, queries.dtype),
        in_specs=[pl.BlockSpec(memory_space=pltpu.VMEM)],
        out_specs=pl.BlockSpec(memory_space=pltpu.VMEM),
        name="finish",
    )(sums)


def solution(mesh):
    count = mesh.shape["ctx"] * mesh.shape["head"]
    by_planes = mesh.shape["head"] == 4 and mesh.shape["ctx"] == 8

    def shards(queries, keys, values):
        if by_planes:
            return planes_path(queries, keys, values, count)
        return ring_path(queries, keys, values, mesh.shape["ctx"])

    spec = P(AXES, None)
    return jax.shard_map(
        shards, mesh=mesh, in_specs=(spec, spec, spec), out_specs=spec, check_vma=False
    )
```

```python
import functools
import math

import jax
import jax.numpy as jnp
from jax import lax
from jax.experimental import pallas as pl
from jax.experimental.pallas import tpu as pltpu
from jax.sharding import PartitionSpec as P

QH = 32
KVH = 4
HD = 128
GROUP = QH // KVH
AXES = ("ctx", "head")
PLANE = 8
FAR = -1e30
FACTOR = math.log2(math.e) / math.sqrt(HD)
VMEM = pl.BlockSpec(memory_space=pltpu.VMEM)
FREE = pl.CostEstimate(flops=0, bytes_accessed=0, transcendentals=0)


def pack_kernel(keys_ref, values_ref, out_ref, sems):
    width = keys_ref.shape[1]
    copies = [
        pltpu.make_async_copy(keys_ref, out_ref.at[:, :width], sems.at[0]),
        pltpu.make_async_copy(values_ref, out_ref.at[:, width:], sems.at[1]),
    ]
    for copy in copies:
        copy.start()
    for copy in copies:
        copy.wait()


def pack(keys, values):
    rows, width = keys.shape
    return pl.pallas_call(
        pack_kernel,
        out_shape=jax.ShapeDtypeStruct((rows, 2 * width), keys.dtype),
        in_specs=[pl.BlockSpec(memory_space=pltpu.HBM)] * 2,
        out_specs=VMEM,
        scratch_shapes=[pltpu.SemaphoreType.DMA((2,))],
        compiler_params=pltpu.CompilerParams(vmem_limit_bytes=2 * 2**20),
        name="pack",
    )(keys, values)


def join_kernel(count, *refs):
    out_ref, rows = refs[-1], 0
    for ref in refs[:count]:
        out_ref[rows : rows + ref.shape[0]] = ref[...]
        rows += ref.shape[0]


def move(kernel, name, blocks, rows, after=()):
    return pl.pallas_call(
        kernel,
        out_shape=jax.ShapeDtypeStruct((rows, blocks[0].shape[1]), blocks[0].dtype),
        in_specs=[VMEM] * len(blocks) + [pl.BlockSpec(memory_space=pl.ANY)] * len(after),
        out_specs=VMEM,
        compiler_params=pltpu.CompilerParams(vmem_limit_bytes=2 * 2**20),
        cost_estimate=FREE,
        name=name,
    )(*blocks, *after)


def join(*blocks, after=()):
    kernel = functools.partial(join_kernel, len(blocks))
    return move(kernel, "join", blocks, sum(b.shape[0] for b in blocks), after)


def hold(block, times=1, after=()):
    for _ in range(times):
        block = join(block, after=after)
    return block


def columns(blocks, at):
    return jnp.concatenate([b[:, at : at + HD] for b in blocks], axis=0)


def weigh(scores, spec, marks):
    if spec not in marks:
        return scores
    if spec[0] == "step":
        return scores + marks[spec]
    rows, cols = marks[spec].shape
    scores = jnp.where(marks[spec][None], scores.reshape(GROUP, rows, cols), FAR)
    return scores.reshape(GROUP * rows, cols)


def make_marks(specs, rows):
    index = lax.axis_index(AXES)
    place, plane = lax.rem(index, PLANE), lax.div(index, PLANE)
    even = lax.rem(place, 2) == 0
    one, two = jnp.where(even, 4, 2), jnp.where(even, 2, 4)
    orders = {"mine": (0, one), "second": (two, 6), "mine_": (1, 1 ^ two), "second_": (1 ^ one, 7)}
    shape = (rows, rows)
    query = place * rows + lax.broadcasted_iota(jnp.int32, shape, 0)
    query = jnp.concatenate([query, query], axis=1)
    key = lax.broadcasted_iota(jnp.int32, shape, 1)
    marks = {}
    for spec in specs:
        if spec[0] == "step":
            marks[spec] = jnp.where((plane ^ spec[1]) < plane, 0.0, FAR)
        else:
            places = [(place ^ o) * rows + key for o in orders[spec[1]]]
            marks[spec] = jnp.concatenate(places, axis=1) <= query
    return marks


def fold_head(h, q_ref, blocks, specs, marks, state):
    queries = jnp.concatenate(
        [q_ref[:, (h * GROUP + g) * HD : (h * GROUP + g + 1) * HD] for g in range(GROUP)], axis=0
    )
    keys = columns(blocks, h * HD)
    values = columns(blocks, (KVH + h) * HD)
    values = jnp.concatenate([values, jnp.ones_like(values)], axis=1)
    scores = lax.dot_general(
        queries, keys, (((1,), (1,)), ((), ())), preferred_element_type=jnp.float32
    )
    parts = [scores[:, at : at + HD] for at in range(0, scores.shape[1], HD)]
    parts = [weigh(part, spec, marks) for part, spec in zip(parts, specs, strict=True)]
    peak = jnp.max(functools.reduce(jnp.maximum, parts), axis=1, keepdims=True)
    peak = jnp.broadcast_to(peak, parts[0].shape)
    if state is not None:
        peak = jnp.maximum(peak, state[0])
    weights = [jnp.exp2((part - peak) * FACTOR).astype(jnp.bfloat16) for part in parts]
    summed = lax.dot_general(
        jnp.concatenate(weights, axis=1), values, (((1,), (0,)), ((), ())),
        preferred_element_type=jnp.float32,
    )
    if state is not None:
        fade = jnp.exp2((state[0] - peak) * FACTOR)
        summed = summed + state[1] * jnp.concatenate([fade, fade], axis=1)
    return peak, summed


def finish_head(h, summed, out_ref):
    result = (summed[:, :HD] / summed[:, HD:]).astype(out_ref.dtype)
    rows = out_ref.shape[0]
    for g in range(GROUP):
        at = (h * GROUP + g) * HD
        out_ref[:, at : at + HD] = result[g * rows : (g + 1) * rows]


def fold_kernel(specs, has_state, last, q_ref, *refs):
    state_refs, refs = (refs[:2], refs[2:]) if has_state else ((), refs)
    blocks, outs = (refs[:-1], refs[-1:]) if last else (refs[:-2], refs[-2:])
    marks = make_marks(specs, q_ref.shape[0])
    steps = {spec for spec in specs if spec[0] == "step"}
    single = len(steps) == 1 and steps == set(specs) and has_state

    def work():
        for h in range(KVH):
            state = tuple(ref[h] for ref in state_refs) or None
            peak, summed = fold_head(h, q_ref, blocks, specs, {} if single else marks, state)
            if last:
                finish_head(h, summed, outs[0])
            else:
                outs[0][h], outs[1][h] = peak, summed

    if not single:
        work()
        return
    valid = marks[specs[0]] == 0.0
    pl.when(valid)(work)
    if last:

        @pl.when(jnp.logical_not(valid))
        def _():
            for h in range(KVH):
                finish_head(h, state_refs[1][h], outs[0])


def state_shapes(rows):
    return (
        jax.ShapeDtypeStruct((KVH, GROUP * rows, HD), jnp.float32),
        jax.ShapeDtypeStruct((KVH, GROUP * rows, 2 * HD), jnp.float32),
    )


def fold(queries, state, pieces, last=False):
    rows = queries.shape[0]
    blocks = [block for block, _ in pieces]
    specs = tuple(spec for _, block_specs in pieces for spec in block_specs)
    operands = [queries, *state, *blocks]
    out_shape = jax.ShapeDtypeStruct(queries.shape, queries.dtype) if last else state_shapes(rows)
    return pl.pallas_call(
        functools.partial(fold_kernel, specs, bool(state), last),
        out_shape=out_shape,
        in_specs=[VMEM] * len(operands),
        out_specs=VMEM if last else (VMEM, VMEM),
        input_output_aliases={1: 0, 2: 1} if state and not last else {},
        compiler_params=pltpu.CompilerParams(vmem_limit_bytes=32 * 2**20),
        cost_estimate=FREE,
        name=f"fold{len(specs)}{'s' if state else 'n'}{'l' if last else ''}",
    )(*operands)


def planes_path(queries, keys, values, count):
    rows = queries.shape[0]
    own = pack(keys, values)

    def exchange(block, even_bits, odd_bits):
        pairs = [(i, i ^ (odd_bits if i % 2 else even_bits)) for i in range(count)]
        return lax.ppermute(block, AXES, pairs)

    def swap(block):
        return exchange(block, 1, 1)

    def double(block, after=()):
        mine = join(block, exchange(block, 4, 2), after=after)
        return mine, exchange(mine, 2, 4)

    group3 = hold(exchange(own, 3 * PLANE, 3 * PLANE), 3)
    group2 = hold(exchange(group3, PLANE, PLANE))
    of_own = (("own", "mine"),), (("own", "second"),), (("own", "mine_"),), (("own", "second_"),)
    of_1, of_2, of_3 = ((("step", step),) for step in (1, 2, 3))

    mine0, second0 = double(own)
    swapped0 = [swap(mine0), swap(second0)]
    state = fold(queries, (), list(zip([mine0, second0], of_own)))
    early = (state[0],)

    mine1, second1 = hold(exchange(mine0, PLANE, PLANE)), exchange(second0, PLANE, PLANE)
    mine3, second3 = double(group3, after=early)
    from1 = [mine1, second1, swap(mine1), swap(second1)]
    from3 = [mine3, second3, swap(mine3), swap(second3)]
    pieces = list(zip(swapped0 + from1 + from3, [*of_own[2:], *[of_1] * 4, *[of_3] * 4]))
    state = fold(queries, state, pieces)

    mine2, second2 = double(group2)
    pieces = [mine2, second2, swap(mine2), swap(hold(second2, after=(state[0],)))]
    return fold(queries, state, [(piece, of_2) for piece in pieces], last=True)


def span_kernel(pos_ref, q_ref, peak_in, sum_in, kv_ref, peak_ref, sum_ref):
    span, rows = kv_ref.shape[0], q_ref.shape[0]
    first, key_first = pos_ref[0], pos_ref[1] + pl.program_id(0) * span

    @pl.when(pl.program_id(0) == 0)
    def _():
        peak_ref[...] = peak_in[...]
        sum_ref[...] = sum_in[...]

    @pl.when((key_first >= 0) & (key_first < first + rows))
    def _():
        shape = (rows, span)
        key_pos = key_first + lax.broadcasted_iota(jnp.int32, shape, 1)
        allowed = key_pos <= first + lax.broadcasted_iota(jnp.int32, shape, 0)
        specs = [("key", at) for at in range(0, span, HD)]
        marks = {spec: allowed[:, spec[1] : spec[1] + HD] for spec in specs}
        for h in range(KVH):
            state = (peak_ref[h], sum_ref[h])
            peak_ref[h], sum_ref[h] = fold_head(h, q_ref, (kv_ref,), specs, marks, state)


def finish_kernel(sum_ref, out_ref):
    for h in range(KVH):
        finish_head(h, sum_ref[h], out_ref)


def ring_path(queries, keys, values, spans):
    rows = queries.shape[0]
    own = pack(keys, values)
    held = lax.all_gather(own, "head", axis=0, tiled=True)
    span_len = held.shape[0]
    span = math.gcd(span_len, 512)
    shapes = state_shapes(rows)
    ctx = lax.axis_index("ctx")
    first = lax.axis_index(AXES) * rows
    whole = [pl.BlockSpec(s.shape, lambda i, d=len(s.shape): (0,) * d) for s in (queries, *shapes)]
    fold = pl.pallas_call(
        span_kernel,
        out_shape=shapes,
        grid=(span_len // span,),
        in_specs=[
            pl.BlockSpec(memory_space=pltpu.SMEM),
            *whole,
            pl.BlockSpec((span, held.shape[1]), lambda i: (i, 0)),
        ],
        out_specs=tuple(whole[1:]),
        compiler_params=pltpu.CompilerParams(vmem_limit_bytes=48 * 2**20),
        name="span",
    )

    def one_step(step, carry):
        held, state = carry
        following = lax.ppermute(held, "ctx", [(i, (i + 1) % spans) for i in range(spans)])
        place = jnp.where(ctx >= step, (ctx - step) * span_len, -span_len)
        state = fold(jnp.stack([first, place]), queries, *state, held)
        return following, tuple(state)

    state = (jnp.full(shapes[0].shape, FAR, jnp.float32), jnp.zeros(shapes[1].shape, jnp.float32))
    sums = lax.fori_loop(0, spans, one_step, (held, state))[1][1]
    return pl.pallas_call(
        finish_kernel,
        out_shape=jax.ShapeDtypeStruct(queries.shape, queries.dtype),
        in_specs=[pl.BlockSpec(memory_space=pltpu.VMEM)],
        out_specs=pl.BlockSpec(memory_space=pltpu.VMEM),
        name="finish",
    )(sums)


def solution(mesh):
    count = mesh.shape["ctx"] * mesh.shape["head"]
    by_planes = mesh.shape["head"] == 4 and mesh.shape["ctx"] == 8

    def shards(queries, keys, values):
        if by_planes:
            return planes_path(queries, keys, values, count)
        return ring_path(queries, keys, values, mesh.shape["ctx"])

    spec = P(AXES, None)
    return jax.shard_map(
        shards, mesh=mesh, in_specs=(spec, spec, spec), out_specs=spec, check_vma=False
    )
```

```python
import functools
import math

import jax
import jax.numpy as jnp
from jax import lax
from jax.experimental import pallas as pl
from jax.experimental.pallas import tpu as pltpu
from jax.sharding import PartitionSpec as P

QH = 32
KVH = 4
HD = 128
GROUP = QH // KVH
AXES = ("ctx", "head")
PLANE = 8
FAR = -1e30
FACTOR = math.log2(math.e) / math.sqrt(HD)
VMEM = pl.BlockSpec(memory_space=pltpu.VMEM)
FREE = pl.CostEstimate(flops=0, bytes_accessed=0, transcendentals=0)


def pack_kernel(keys_ref, values_ref, out_ref, sems):
    width = keys_ref.shape[1]
    copies = [
        pltpu.make_async_copy(keys_ref, out_ref.at[:, :width], sems.at[0]),
        pltpu.make_async_copy(values_ref, out_ref.at[:, width:], sems.at[1]),
    ]
    for copy in copies:
        copy.start()
    for copy in copies:
        copy.wait()


def pack(keys, values):
    rows, width = keys.shape
    return pl.pallas_call(
        pack_kernel,
        out_shape=jax.ShapeDtypeStruct((rows, 2 * width), keys.dtype),
        in_specs=[pl.BlockSpec(memory_space=pltpu.HBM)] * 2,
        out_specs=VMEM,
        scratch_shapes=[pltpu.SemaphoreType.DMA((2,))],
        compiler_params=pltpu.CompilerParams(vmem_limit_bytes=2 * 2**20),
        name="pack",
    )(keys, values)


def stage_kernel(queries_ref, own_ref, out_ref, sem):
    copy = pltpu.make_async_copy(queries_ref, out_ref, sem)
    copy.start()
    copy.wait()


def stage(queries, own):
    return pl.pallas_call(
        stage_kernel,
        out_shape=jax.ShapeDtypeStruct(queries.shape, queries.dtype),
        in_specs=[pl.BlockSpec(memory_space=pltpu.HBM), pl.BlockSpec(memory_space=pl.ANY)],
        out_specs=VMEM,
        scratch_shapes=[pltpu.SemaphoreType.DMA(())],
        compiler_params=pltpu.CompilerParams(vmem_limit_bytes=2 * 2**20),
        cost_estimate=FREE,
        name="stage",
    )(queries, own)


def join_kernel(count, *refs):
    out_ref, rows = refs[-1], 0
    for ref in refs[:count]:
        out_ref[rows : rows + ref.shape[0]] = ref[...]
        rows += ref.shape[0]


def move(kernel, name, blocks, rows, after=()):
    return pl.pallas_call(
        kernel,
        out_shape=jax.ShapeDtypeStruct((rows, blocks[0].shape[1]), blocks[0].dtype),
        in_specs=[VMEM] * len(blocks) + [pl.BlockSpec(memory_space=pl.ANY)] * len(after),
        out_specs=VMEM,
        compiler_params=pltpu.CompilerParams(vmem_limit_bytes=2 * 2**20),
        cost_estimate=FREE,
        name=name,
    )(*blocks, *after)


def join(*blocks, after=()):
    kernel = functools.partial(join_kernel, len(blocks))
    return move(kernel, "join", blocks, sum(b.shape[0] for b in blocks), after)


def hold(block, times=1, after=()):
    for _ in range(times):
        block = join(block, after=after)
    return block


def columns(blocks, at):
    return jnp.concatenate([b[:, at : at + HD] for b in blocks], axis=0)


def weigh(scores, spec, marks):
    if spec not in marks:
        return scores
    if spec[0] == "step":
        return scores + marks[spec]
    rows, cols = marks[spec].shape
    scores = jnp.where(marks[spec][None], scores.reshape(GROUP, rows, cols), FAR)
    return scores.reshape(GROUP * rows, cols)


def make_marks(specs, rows):
    index = lax.axis_index(AXES)
    place, plane = lax.rem(index, PLANE), lax.div(index, PLANE)
    even = lax.rem(place, 2) == 0
    one, two = jnp.where(even, 4, 2), jnp.where(even, 2, 4)
    orders = {"mine": (0, one), "second": (two, 6), "mine_": (1, 1 ^ two), "second_": (1 ^ one, 7)}
    shape = (rows, rows)
    query = place * rows + lax.broadcasted_iota(jnp.int32, shape, 0)
    query = jnp.concatenate([query, query], axis=1)
    key = lax.broadcasted_iota(jnp.int32, shape, 1)
    marks = {}
    for spec in specs:
        if spec[0] == "step":
            marks[spec] = jnp.where((plane ^ spec[1]) < plane, 0.0, FAR)
        else:
            places = [(place ^ o) * rows + key for o in orders[spec[1]]]
            marks[spec] = jnp.concatenate(places, axis=1) <= query
    return marks


def fold_head(h, q_ref, blocks, specs, marks, state):
    queries = jnp.concatenate(
        [q_ref[:, (h * GROUP + g) * HD : (h * GROUP + g + 1) * HD] for g in range(GROUP)], axis=0
    )
    keys = columns(blocks, h * HD)
    values = columns(blocks, (KVH + h) * HD)
    values = jnp.concatenate([values, jnp.ones_like(values)], axis=1)
    scores = lax.dot_general(
        queries, keys, (((1,), (1,)), ((), ())), preferred_element_type=jnp.float32
    )
    parts = [scores[:, at : at + HD] for at in range(0, scores.shape[1], HD)]
    parts = [weigh(part, spec, marks) for part, spec in zip(parts, specs, strict=True)]
    peak = jnp.max(functools.reduce(jnp.maximum, parts), axis=1, keepdims=True)
    peak = jnp.broadcast_to(peak, parts[0].shape)
    if state is not None:
        peak = jnp.maximum(peak, state[0])
    weights = [jnp.exp2((part - peak) * FACTOR).astype(jnp.bfloat16) for part in parts]
    summed = lax.dot_general(
        jnp.concatenate(weights, axis=1), values, (((1,), (0,)), ((), ())),
        preferred_element_type=jnp.float32,
    )
    if state is not None:
        fade = jnp.exp2((state[0] - peak) * FACTOR)
        summed = summed + state[1] * jnp.concatenate([fade, fade], axis=1)
    return peak, summed


def finish_head(h, summed, out_ref):
    result = (summed[:, :HD] / summed[:, HD:]).astype(out_ref.dtype)
    rows = out_ref.shape[0]
    for g in range(GROUP):
        at = (h * GROUP + g) * HD
        out_ref[:, at : at + HD] = result[g * rows : (g + 1) * rows]


def fold_kernel(specs, has_state, last, q_ref, *refs):
    state_refs, refs = (refs[:2], refs[2:]) if has_state else ((), refs)
    blocks, outs = (refs[:-1], refs[-1:]) if last else (refs[:-2], refs[-2:])
    marks = make_marks(specs, q_ref.shape[0])
    steps = {spec for spec in specs if spec[0] == "step"}
    single = len(steps) == 1 and steps == set(specs) and has_state

    def work():
        for h in range(KVH):
            state = tuple(ref[h] for ref in state_refs) or None
            peak, summed = fold_head(h, q_ref, blocks, specs, {} if single else marks, state)
            if last:
                finish_head(h, summed, outs[0])
            else:
                outs[0][h], outs[1][h] = peak, summed

    if not single:
        work()
        return
    valid = marks[specs[0]] == 0.0
    pl.when(valid)(work)
    if last:

        @pl.when(jnp.logical_not(valid))
        def _():
            for h in range(KVH):
                finish_head(h, state_refs[1][h], outs[0])


def state_shapes(rows):
    return (
        jax.ShapeDtypeStruct((KVH, GROUP * rows, HD), jnp.float32),
        jax.ShapeDtypeStruct((KVH, GROUP * rows, 2 * HD), jnp.float32),
    )


def fold(queries, state, pieces, last=False):
    rows = queries.shape[0]
    blocks = [block for block, _ in pieces]
    specs = tuple(spec for _, block_specs in pieces for spec in block_specs)
    operands = [queries, *state, *blocks]
    out_shape = jax.ShapeDtypeStruct(queries.shape, queries.dtype) if last else state_shapes(rows)
    return pl.pallas_call(
        functools.partial(fold_kernel, specs, bool(state), last),
        out_shape=out_shape,
        in_specs=[VMEM] * len(operands),
        out_specs=VMEM if last else (VMEM, VMEM),
        input_output_aliases={1: 0, 2: 1} if state and not last else {},
        compiler_params=pltpu.CompilerParams(vmem_limit_bytes=32 * 2**20),
        cost_estimate=FREE,
        name=f"fold{len(specs)}{'s' if state else 'n'}{'l' if last else ''}",
    )(*operands)


def planes_path(queries, keys, values, count):
    rows = queries.shape[0]
    own = pack(keys, values)
    queries = stage(queries, own)

    def exchange(block, even_bits, odd_bits):
        pairs = [(i, i ^ (odd_bits if i % 2 else even_bits)) for i in range(count)]
        return lax.ppermute(block, AXES, pairs)

    def swap(block):
        return exchange(block, 1, 1)

    def double(block, after=()):
        mine = join(block, exchange(block, 4, 2), after=after)
        return mine, exchange(mine, 2, 4)

    group3 = hold(exchange(own, 3 * PLANE, 3 * PLANE), 3)
    group2 = hold(exchange(group3, PLANE, PLANE))
    of_own = (("own", "mine"),), (("own", "second"),), (("own", "mine_"),), (("own", "second_"),)
    of_1, of_2, of_3 = ((("step", step),) for step in (1, 2, 3))

    mine0, second0 = double(own)
    swapped0 = [swap(mine0), swap(second0)]
    state = fold(queries, (), list(zip([mine0, second0], of_own)))
    early = (state[0],)

    mine1, second1 = hold(exchange(mine0, PLANE, PLANE)), exchange(second0, PLANE, PLANE)
    mine3, second3 = double(group3, after=early)
    from1 = [mine1, second1, swap(mine1), swap(second1)]
    from3 = [mine3, second3, swap(mine3), swap(second3)]
    pieces = list(zip(swapped0 + from1 + from3, [*of_own[2:], *[of_1] * 4, *[of_3] * 4]))
    state = fold(queries, state, pieces)

    mine2, second2 = double(group2)
    pieces = [mine2, second2, swap(mine2), swap(hold(second2, after=(state[0],)))]
    return fold(queries, state, [(piece, of_2) for piece in pieces], last=True)


def span_kernel(pos_ref, q_ref, peak_in, sum_in, kv_ref, peak_ref, sum_ref):
    span, rows = kv_ref.shape[0], q_ref.shape[0]
    first, key_first = pos_ref[0], pos_ref[1] + pl.program_id(0) * span

    @pl.when(pl.program_id(0) == 0)
    def _():
        peak_ref[...] = peak_in[...]
        sum_ref[...] = sum_in[...]

    @pl.when((key_first >= 0) & (key_first < first + rows))
    def _():
        shape = (rows, span)
        key_pos = key_first + lax.broadcasted_iota(jnp.int32, shape, 1)
        allowed = key_pos <= first + lax.broadcasted_iota(jnp.int32, shape, 0)
        specs = [("key", at) for at in range(0, span, HD)]
        marks = {spec: allowed[:, spec[1] : spec[1] + HD] for spec in specs}
        for h in range(KVH):
            state = (peak_ref[h], sum_ref[h])
            peak_ref[h], sum_ref[h] = fold_head(h, q_ref, (kv_ref,), specs, marks, state)


def finish_kernel(sum_ref, out_ref):
    for h in range(KVH):
        finish_head(h, sum_ref[h], out_ref)


def ring_path(queries, keys, values, spans):
    rows = queries.shape[0]
    own = pack(keys, values)
    held = lax.all_gather(own, "head", axis=0, tiled=True)
    span_len = held.shape[0]
    span = math.gcd(span_len, 512)
    shapes = state_shapes(rows)
    ctx = lax.axis_index("ctx")
    first = lax.axis_index(AXES) * rows
    whole = [pl.BlockSpec(s.shape, lambda i, d=len(s.shape): (0,) * d) for s in (queries, *shapes)]
    fold = pl.pallas_call(
        span_kernel,
        out_shape=shapes,
        grid=(span_len // span,),
        in_specs=[
            pl.BlockSpec(memory_space=pltpu.SMEM),
            *whole,
            pl.BlockSpec((span, held.shape[1]), lambda i: (i, 0)),
        ],
        out_specs=tuple(whole[1:]),
        compiler_params=pltpu.CompilerParams(vmem_limit_bytes=48 * 2**20),
        name="span",
    )

    def one_step(step, carry):
        held, state = carry
        following = lax.ppermute(held, "ctx", [(i, (i + 1) % spans) for i in range(spans)])
        place = jnp.where(ctx >= step, (ctx - step) * span_len, -span_len)
        state = fold(jnp.stack([first, place]), queries, *state, held)
        return following, tuple(state)

    state = (jnp.full(shapes[0].shape, FAR, jnp.float32), jnp.zeros(shapes[1].shape, jnp.float32))
    sums = lax.fori_loop(0, spans, one_step, (held, state))[1][1]
    return pl.pallas_call(
        finish_kernel,
        out_shape=jax.ShapeDtypeStruct(queries.shape, queries.dtype),
        in_specs=[pl.BlockSpec(memory_space=pltpu.VMEM)],
        out_specs=pl.BlockSpec(memory_space=pltpu.VMEM),
        name="finish",
    )(sums)


def solution(mesh):
    count = mesh.shape["ctx"] * mesh.shape["head"]
    by_planes = mesh.shape["head"] == 4 and mesh.shape["ctx"] == 8

    def shards(queries, keys, values):
        if by_planes:
            return planes_path(queries, keys, values, count)
        return ring_path(queries, keys, values, mesh.shape["ctx"])

    spec = P(AXES, None)
    return jax.shard_map(
        shards, mesh=mesh, in_specs=(spec, spec, spec), out_specs=spec, check_vma=False
    )
```

```python
import functools
import math

import jax
import jax.numpy as jnp
from jax import lax
from jax.experimental import pallas as pl
from jax.experimental.pallas import tpu as pltpu
from jax.sharding import PartitionSpec as P

QH = 32
KVH = 4
HD = 128
GROUP = QH // KVH
AXES = ("ctx", "head")
PLANE = 8
FAR = -1e30
FACTOR = math.log2(math.e) / math.sqrt(HD)
VMEM = pl.BlockSpec(memory_space=pltpu.VMEM)
FREE = pl.CostEstimate(flops=0, bytes_accessed=0, transcendentals=0)


def pack_kernel(keys_ref, values_ref, out_ref, sems):
    width = keys_ref.shape[1]
    copies = [
        pltpu.make_async_copy(keys_ref, out_ref.at[:, :width], sems.at[0]),
        pltpu.make_async_copy(values_ref, out_ref.at[:, width:], sems.at[1]),
    ]
    for copy in copies:
        copy.start()
    for copy in copies:
        copy.wait()


def pack(keys, values):
    rows, width = keys.shape
    return pl.pallas_call(
        pack_kernel,
        out_shape=jax.ShapeDtypeStruct((rows, 2 * width), keys.dtype),
        in_specs=[pl.BlockSpec(memory_space=pltpu.HBM)] * 2,
        out_specs=VMEM,
        scratch_shapes=[pltpu.SemaphoreType.DMA((2,))],
        compiler_params=pltpu.CompilerParams(vmem_limit_bytes=2 * 2**20),
        name="pack",
    )(keys, values)


def stage_kernel(queries_ref, own_ref, out_ref, sem):
    copy = pltpu.make_async_copy(queries_ref, out_ref, sem)
    copy.start()
    copy.wait()


def stage(queries, own):
    return pl.pallas_call(
        stage_kernel,
        out_shape=jax.ShapeDtypeStruct(queries.shape, queries.dtype),
        in_specs=[pl.BlockSpec(memory_space=pltpu.HBM), pl.BlockSpec(memory_space=pl.ANY)],
        out_specs=VMEM,
        scratch_shapes=[pltpu.SemaphoreType.DMA(())],
        compiler_params=pltpu.CompilerParams(vmem_limit_bytes=2 * 2**20),
        cost_estimate=FREE,
        name="stage",
    )(queries, own)


def join_kernel(count, *refs):
    out_ref, rows = refs[-1], 0
    for ref in refs[:count]:
        out_ref[rows : rows + ref.shape[0]] = ref[...]
        rows += ref.shape[0]


def move(kernel, name, blocks, rows, after=()):
    return pl.pallas_call(
        kernel,
        out_shape=jax.ShapeDtypeStruct((rows, blocks[0].shape[1]), blocks[0].dtype),
        in_specs=[VMEM] * len(blocks) + [pl.BlockSpec(memory_space=pl.ANY)] * len(after),
        out_specs=VMEM,
        compiler_params=pltpu.CompilerParams(vmem_limit_bytes=2 * 2**20),
        cost_estimate=FREE,
        name=name,
    )(*blocks, *after)


def join(*blocks, after=()):
    kernel = functools.partial(join_kernel, len(blocks))
    return move(kernel, "join", blocks, sum(b.shape[0] for b in blocks), after)


def hold(block, times=1, after=()):
    for _ in range(times):
        block = join(block, after=after)
    return block


def columns(blocks, at):
    return jnp.concatenate([b[:, at : at + HD] for b in blocks], axis=0)


def weigh(scores, spec, marks):
    if spec not in marks:
        return scores
    if spec[0] == "step":
        return scores + marks[spec]
    rows, cols = marks[spec].shape
    scores = jnp.where(marks[spec][None], scores.reshape(GROUP, rows, cols), FAR)
    return scores.reshape(GROUP * rows, cols)


def make_marks(specs, rows):
    index = lax.axis_index(AXES)
    place, plane = lax.rem(index, PLANE), lax.div(index, PLANE)
    even = lax.rem(place, 2) == 0
    one, two = jnp.where(even, 4, 2), jnp.where(even, 2, 4)
    orders = {"mine": (0, one), "second": (two, 6), "mine_": (1, 1 ^ two), "second_": (1 ^ one, 7)}
    shape = (rows, rows)
    query = place * rows + lax.broadcasted_iota(jnp.int32, shape, 0)
    query = jnp.concatenate([query, query], axis=1)
    key = lax.broadcasted_iota(jnp.int32, shape, 1)
    marks = {}
    for spec in specs:
        if spec[0] == "step":
            marks[spec] = jnp.where((plane ^ spec[1]) < plane, 0.0, FAR)
        else:
            places = [(place ^ o) * rows + key for o in orders[spec[1]]]
            marks[spec] = jnp.concatenate(places, axis=1) <= query
    return marks


def fold_head(h, q_ref, blocks, specs, marks, state):
    queries = jnp.concatenate(
        [q_ref[:, (h * GROUP + g) * HD : (h * GROUP + g + 1) * HD] for g in range(GROUP)], axis=0
    )
    keys = columns(blocks, h * HD)
    values = columns(blocks, (KVH + h) * HD)
    values = jnp.concatenate([values, jnp.ones_like(values)], axis=1)
    scores = lax.dot_general(
        queries, keys, (((1,), (1,)), ((), ())), preferred_element_type=jnp.float32
    )
    parts = [scores[:, at : at + HD] for at in range(0, scores.shape[1], HD)]
    parts = [weigh(part, spec, marks) for part, spec in zip(parts, specs, strict=True)]
    peak = jnp.max(functools.reduce(jnp.maximum, parts), axis=1, keepdims=True)
    peak = jnp.broadcast_to(peak, parts[0].shape)
    if state is not None:
        peak = jnp.maximum(peak, state[0])
    weights = [jnp.exp2((part - peak) * FACTOR).astype(jnp.bfloat16) for part in parts]
    summed = lax.dot_general(
        jnp.concatenate(weights, axis=1), values, (((1,), (0,)), ((), ())),
        preferred_element_type=jnp.float32,
    )
    if state is not None:
        fade = jnp.exp2((state[0] - peak) * FACTOR)
        summed = summed + state[1] * jnp.concatenate([fade, fade], axis=1)
    return peak, summed


def finish_head(h, summed, out_ref):
    result = (summed[:, :HD] / summed[:, HD:]).astype(out_ref.dtype)
    rows = out_ref.shape[0]
    for g in range(GROUP):
        at = (h * GROUP + g) * HD
        out_ref[:, at : at + HD] = result[g * rows : (g + 1) * rows]


def fold_kernel(specs, has_state, last, q_ref, *refs):
    state_refs, refs = (refs[:2], refs[2:]) if has_state else ((), refs)
    blocks, outs = (refs[:-1], refs[-1:]) if last else (refs[:-2], refs[-2:])
    marks = make_marks(specs, q_ref.shape[0])
    steps = {spec for spec in specs if spec[0] == "step"}
    single = len(steps) == 1 and steps == set(specs) and has_state

    def work(some=None, state_from=state_refs, used=None):
        some = range(len(specs)) if some is None else some
        some_blocks, some_specs = [blocks[i] for i in some], [specs[i] for i in some]
        used = ({} if single else marks) if used is None else used
        for h in range(KVH):
            state = tuple(ref[h] for ref in state_from) or None
            peak, summed = fold_head(h, q_ref, some_blocks, some_specs, used, state)
            if last:
                finish_head(h, summed, outs[0])
            else:
                outs[0][h], outs[1][h] = peak, summed

    if len(steps) > 1 and has_state and not last:
        own_marks = {spec: mark for spec, mark in marks.items() if spec not in steps}
        valid = {spec: marks[spec] == 0.0 for spec in sorted(steps)}
        every = functools.reduce(jnp.logical_and, valid.values())
        pl.when(every)(lambda: work(used=own_marks))

        @pl.when(jnp.logical_not(every))
        def _():
            work([i for i, spec in enumerate(specs) if spec not in steps], used=own_marks)
            for step, earlier in valid.items():
                some = [i for i, spec in enumerate(specs) if spec == step]
                pl.when(earlier)(functools.partial(work, some, outs, own_marks))

        return

    if not single:
        work()
        return
    valid = marks[specs[0]] == 0.0
    pl.when(valid)(work)
    if last:

        @pl.when(jnp.logical_not(valid))
        def _():
            for h in range(KVH):
                finish_head(h, state_refs[1][h], outs[0])


def state_shapes(rows):
    return (
        jax.ShapeDtypeStruct((KVH, GROUP * rows, HD), jnp.float32),
        jax.ShapeDtypeStruct((KVH, GROUP * rows, 2 * HD), jnp.float32),
    )


def fold(queries, state, pieces, last=False):
    rows = queries.shape[0]
    blocks = [block for block, _ in pieces]
    specs = tuple(spec for _, block_specs in pieces for spec in block_specs)
    operands = [queries, *state, *blocks]
    out_shape = jax.ShapeDtypeStruct(queries.shape, queries.dtype) if last else state_shapes(rows)
    return pl.pallas_call(
        functools.partial(fold_kernel, specs, bool(state), last),
        out_shape=out_shape,
        in_specs=[VMEM] * len(operands),
        out_specs=VMEM if last else (VMEM, VMEM),
        input_output_aliases={1: 0, 2: 1} if state and not last else {},
        compiler_params=pltpu.CompilerParams(vmem_limit_bytes=32 * 2**20),
        cost_estimate=FREE,
        name=f"fold{len(specs)}{'s' if state else 'n'}{'l' if last else ''}",
    )(*operands)


def planes_path(queries, keys, values, count):
    rows = queries.shape[0]
    own = pack(keys, values)
    queries = stage(queries, own)

    def exchange(block, even_bits, odd_bits):
        pairs = [(i, i ^ (odd_bits if i % 2 else even_bits)) for i in range(count)]
        return lax.ppermute(block, AXES, pairs)

    def swap(block):
        return exchange(block, 1, 1)

    def double(block, after=()):
        mine = join(block, exchange(block, 4, 2), after=after)
        return mine, exchange(mine, 2, 4)

    group3 = hold(exchange(own, 3 * PLANE, 3 * PLANE), 3)
    group2 = hold(exchange(group3, PLANE, PLANE))
    of_own = (("own", "mine"),), (("own", "second"),), (("own", "mine_"),), (("own", "second_"),)
    of_1, of_2, of_3 = ((("step", step),) for step in (1, 2, 3))

    mine0, second0 = double(own)
    swapped0 = [swap(mine0), swap(second0)]
    state = fold(queries, (), list(zip([mine0, second0], of_own)))
    early = (state[0],)

    mine1, second1 = hold(exchange(mine0, PLANE, PLANE)), exchange(second0, PLANE, PLANE)
    mine3, second3 = double(group3, after=early)
    from1 = [mine1, second1, swap(mine1), swap(second1)]
    from3 = [mine3, second3, swap(mine3), swap(second3)]
    pieces = list(zip(swapped0 + from1 + from3, [*of_own[2:], *[of_1] * 4, *[of_3] * 4]))
    state = fold(queries, state, pieces)

    mine2, second2 = double(group2)
    pieces = [mine2, second2, swap(mine2), swap(hold(second2, after=(state[0],)))]
    return fold(queries, state, [(piece, of_2) for piece in pieces], last=True)


def span_kernel(pos_ref, q_ref, peak_in, sum_in, kv_ref, peak_ref, sum_ref):
    span, rows = kv_ref.shape[0], q_ref.shape[0]
    first, key_first = pos_ref[0], pos_ref[1] + pl.program_id(0) * span

    @pl.when(pl.program_id(0) == 0)
    def _():
        peak_ref[...] = peak_in[...]
        sum_ref[...] = sum_in[...]

    @pl.when((key_first >= 0) & (key_first < first + rows))
    def _():
        shape = (rows, span)
        key_pos = key_first + lax.broadcasted_iota(jnp.int32, shape, 1)
        allowed = key_pos <= first + lax.broadcasted_iota(jnp.int32, shape, 0)
        specs = [("key", at) for at in range(0, span, HD)]
        marks = {spec: allowed[:, spec[1] : spec[1] + HD] for spec in specs}
        for h in range(KVH):
            state = (peak_ref[h], sum_ref[h])
            peak_ref[h], sum_ref[h] = fold_head(h, q_ref, (kv_ref,), specs, marks, state)


def finish_kernel(sum_ref, out_ref):
    for h in range(KVH):
        finish_head(h, sum_ref[h], out_ref)


def ring_path(queries, keys, values, spans):
    rows = queries.shape[0]
    own = pack(keys, values)
    held = lax.all_gather(own, "head", axis=0, tiled=True)
    span_len = held.shape[0]
    span = math.gcd(span_len, 512)
    shapes = state_shapes(rows)
    ctx = lax.axis_index("ctx")
    first = lax.axis_index(AXES) * rows
    whole = [pl.BlockSpec(s.shape, lambda i, d=len(s.shape): (0,) * d) for s in (queries, *shapes)]
    fold = pl.pallas_call(
        span_kernel,
        out_shape=shapes,
        grid=(span_len // span,),
        in_specs=[
            pl.BlockSpec(memory_space=pltpu.SMEM),
            *whole,
            pl.BlockSpec((span, held.shape[1]), lambda i: (i, 0)),
        ],
        out_specs=tuple(whole[1:]),
        compiler_params=pltpu.CompilerParams(vmem_limit_bytes=48 * 2**20),
        name="span",
    )

    def one_step(step, carry):
        held, state = carry
        following = lax.ppermute(held, "ctx", [(i, (i + 1) % spans) for i in range(spans)])
        place = jnp.where(ctx >= step, (ctx - step) * span_len, -span_len)
        state = fold(jnp.stack([first, place]), queries, *state, held)
        return following, tuple(state)

    state = (jnp.full(shapes[0].shape, FAR, jnp.float32), jnp.zeros(shapes[1].shape, jnp.float32))
    sums = lax.fori_loop(0, spans, one_step, (held, state))[1][1]
    return pl.pallas_call(
        finish_kernel,
        out_shape=jax.ShapeDtypeStruct(queries.shape, queries.dtype),
        in_specs=[pl.BlockSpec(memory_space=pltpu.VMEM)],
        out_specs=pl.BlockSpec(memory_space=pltpu.VMEM),
        name="finish",
    )(sums)


def solution(mesh):
    count = mesh.shape["ctx"] * mesh.shape["head"]
    by_planes = mesh.shape["head"] == 4 and mesh.shape["ctx"] == 8

    def shards(queries, keys, values):
        if by_planes:
            return planes_path(queries, keys, values, count)
        return ring_path(queries, keys, values, mesh.shape["ctx"])

    spec = P(AXES, None)
    return jax.shard_map(
        shards, mesh=mesh, in_specs=(spec, spec, spec), out_specs=spec, check_vma=False
    )
```
